128 devices in a mesh: replica: 8 (over x, core), shard: 16 (over z, y).
Axes of the slice: x: 4, y: 4, z: 4, core: 2. Of those that a mesh axis runs over, the one named last changes fastest.
Arguments:
- activations: bfloat16 [32768, 4096], P(('replica', 'shard')), may hold values from -6 to 6
- output_grads: bfloat16 [32768, 8192], P('replica', 'shard'), may hold values from -0.099609375 to 0.099609375
- error_buffer: float32 [8, 4096, 8192], P('replica', None, 'shard'), may hold values from -3 to 3
- previous_factor: float32 [8192, 32], P('shard'), may hold values from -0.0625 to 0.0625
Outputs:
- new_errors: float32 [8, 4096, 8192], P('replica', None, 'shard')
- basis: float32 [4096, 32], replicated
- right_factor: float32 [8192, 32], P('shard')
The draws below stay inside these ranges and needn't reach their ends.
All inputs are finite; a program needn't handle non-finite values.
Results may differ from the reference program's by a relative error of at most 0.0003.
Values may be sent and summed in bfloat16 or wider, within the bound.
No kernel may reach another device: no remote copies, remote signals or barrier semaphores. Data moves between devices by JAX's collectives and lax.ppermute only.
A program may use at most 128 MiB of HBM per device.

```python
import jax
import jax.numpy as jnp
from jax import lax

D = 4096
HID = 8192
RANK = 32
REPLICAS = 8
TOKENS = 32768
N_REPLICA = 8


def block_levels(key, shape, split, smallest, high):
    factor_of, own = 1.0, jax.random.fold_in(key, 6)
    for position, parts in split:
        heights = jnp.exp(jax.random.uniform(jax.random.fold_in(own, position), (parts,), jnp.float32, smallest / len(split), high / len(split)))
        factor_of = factor_of * jnp.repeat(heights, shape[position] // parts).reshape([-1 if axis == position else 1 for axis in range(len(shape))])
    return factor_of


def centred(own_key, dims, deviation, reach, split=(), held_as=jnp.bfloat16):
    drawn = jax.random.normal(own_key, dims, jnp.float32) * deviation
    if len(split) > 0:
        drawn = block_levels(own_key, dims, split, -0.22, 0.18) * drawn
    return jnp.clip(drawn, min=-reach, max=reach).astype(held_as)


def setup_inputs(seed: int = 0) -> dict:
    arg_keys = jax.random.split(jax.random.key(seed), 5)
    return {
        "activations": centred(arg_keys[0], (TOKENS, D), 1.0, 6.0, ((0, 128),)),
        "output_grads": centred(arg_keys[1], (TOKENS, HID), 0.015625, 0.099609375, ((0, 8), (1, 16))),
        "error_buffer": centred(arg_keys[2], (REPLICAS, D, HID), 0.5, 3.0, ((0, 8), (2, 16)), jnp.float32),
        "previous_factor": centred(arg_keys[3], (HID, RANK), HID ** -0.5, 0.0625, ((0, 16),), jnp.float32),
    }


def reference(activations, output_grads, error_buffer, previous_factor):
    inputs_all = activations.reshape(N_REPLICA, -1, D)
    grads_all = output_grads.reshape(N_REPLICA, -1, HID)
    matrices = []
    for replica in range(N_REPLICA):
        grad = jnp.dot(inputs_all[replica].T.astype(jnp.float32), grads_all[replica].astype(jnp.float32), preferred_element_type=jnp.float32)
        matrices.append(error_buffer[replica] + grad)
    left = jnp.zeros((D, RANK), jnp.float32)
    for matrix in matrices:
        left = left + jnp.dot(matrix, previous_factor, precision=lax.Precision.HIGHEST)
    gram = jnp.dot(left.T, left, precision=lax.Precision.HIGHEST)
    lower_factor = jnp.linalg.cholesky(gram)
    basis = lax.linalg.triangular_solve(lower_factor, left, left_side=False, lower=True, transpose_a=True)
    right_factor = jnp.zeros((HID, RANK), jnp.float32)
    for matrix in matrices:
        right_factor = right_factor + jnp.dot(matrix.T, basis, precision=lax.Precision.HIGHEST)
    right_factor = right_factor / N_REPLICA
    update = jnp.dot(basis, right_factor.T, precision=lax.Precision.HIGHEST)
    new_errors = jnp.stack([matrix - update for matrix in matrices])
    return (new_errors, basis, right_factor)
```

```python
import jax
import jax.numpy as jnp
from jax import lax
from jax.sharding import PartitionSpec as P

ALL = ("replica", "shard")
NX, NC, NZ, NY = 4, 2, 4, 4
HI = lax.Precision.HIGHEST


def pairs(move):
    out = []
    for x in range(NX):
        for c in range(NC):
            for z in range(NZ):
                for y in range(NY):
                    a, b, d, e = move(x, c, z, y)
                    out.append((((x * NC + c) * NZ + z) * NY + y, ((a * NC + b) * NZ + d) * NY + e))
    return out


def inner(v):
    return v ^ 1


def outer(v):
    return 3 - v


def on_p(f):
    return pairs(lambda x, c, z, y: (x, c, z, f(y)) if c == 0 else (x, c, f(z), y))


def on_q(f):
    return pairs(lambda x, c, z, y: (x, c, f(z), y) if c == 0 else (x, c, z, f(y)))


PIN, POUT, QIN, QOUT = on_p(inner), on_p(outer), on_q(inner), on_q(outer)
XIN = pairs(lambda x, c, z, y: (inner(x), c, z, y))
XOUT = pairs(lambda x, c, z, y: (outer(x), c, z, y))
CORE = pairs(lambda x, c, z, y: (x, 1 - c, z, y))


def send(a, perm):
    return lax.ppermute(a, ALL, perm)


def split3(a):
    hi = lax.reduce_precision(a, 8, 7)
    mid = lax.reduce_precision(a - hi, 8, 7)
    lo = lax.reduce_precision(a - hi - mid, 8, 7)
    return jnp.concatenate([hi, mid, lo], 0).astype(jnp.bfloat16)


def exact_dot(a32, b16, dims):
    r = lax.dot_general(split3(a32), b16, (dims, ((), ())), preferred_element_type=jnp.float32)
    n = a32.shape[0]
    return r[:n] + r[n : 2 * n] + r[2 * n :]


def halve(a, bit, perm):
    mine = jnp.where(bit, a[1], a[0])
    other = jnp.where(bit, a[0], a[1])
    return mine + send(other, perm)


def double(a, bit, perm):
    b = send(a, perm)
    return jnp.where(bit, jnp.stack([b, a]), jnp.stack([a, b]))


def by_code(a):
    return a[jnp.array([0, 1, 3, 2])].reshape((2, 2) + a.shape[1:])


def local(activations, output_grads, error_buffer, previous_factor):
    errors = error_buffer[0]
    rep, sh = lax.axis_index("replica"), lax.axis_index("shard")
    x, core = rep // 2, rep % 2
    z, y = sh // 4, sh % 4
    p = jnp.where(core == 0, y, z)
    q = jnp.where(core == 0, z, y)

    def bits(v):
        return v // 2 == 1, (v == 1) | (v == 2)

    (hp, cp), (hq, cq), (hx, cx) = bits(p), bits(q), bits(x)

    gathered = lax.all_gather(activations, "shard", axis=0, tiled=True)

    factor_t = previous_factor.T
    u = exact_dot(factor_t, output_grads, ((1,), (1,)))
    u = u.reshape(32, 4, 4, 256).transpose(1, 2, 0, 3)
    u = jnp.where(core == 0, u, u.swapaxes(0, 1))
    u = u[jnp.array([0, 1, 3, 2])][:, jnp.array([0, 1, 3, 2])].reshape(2, 2, 2, 2, 32, 256)
    u = halve(u, hq, QOUT)
    u = halve(u.swapaxes(0, 1), hp, POUT)
    u = halve(u, cq, QIN)
    u = halve(u, cp, PIN)

    left = exact_dot(u, activations, ((1,), (0,)))
    left = left + lax.dot_general(factor_t, errors, (((1,), (1,)), ((), ())), precision=HI)
    left = left.reshape(32, 8, 512).swapaxes(0, 1).reshape(2, 2, 2, 32, 512)
    left = halve(left, core == 1, CORE)
    left = halve(left, hx, XOUT)
    left = halve(left, cx, XIN)
    for perm in (PIN, QIN, POUT, QOUT):
        left = left + send(left, perm)
    left = double(left, cx, XIN)
    left = double(left, hx, XOUT)
    left = double(left, core == 1, CORE).reshape(8, 32, 512)
    left = left.swapaxes(0, 1).reshape(32, 4096)

    gram = lax.dot_general(left, left, (((1,), (1,)), ((), ())), precision=HI)
    lower_factor = jnp.linalg.cholesky(gram)
    basis = lax.linalg.triangular_solve(lower_factor, left, left_side=True, lower=True)

    w = lax.dot_general(split3(basis), activations, (((1,), (1,)), ((), ())), preferred_element_type=jnp.float32)
    w = w[:32] + w[32:64] + w[64:]
    w = double(w, cp, PIN)
    w = double(w, cq, QIN)
    w = double(w, hp, POUT)
    w = double(w, hq, QOUT)
    w = w.swapaxes(1, 2).reshape(4, 4, 32, 256)[jnp.array([0, 1, 3, 2])][:, jnp.array([0, 1, 3, 2])]
    w = jnp.where(core == 0, w, w.swapaxes(0, 1))
    w = w.transpose(2, 0, 1, 3).reshape(32, 4096)
    right = exact_dot(w, output_grads, ((1,), (0,)))
    right = right + lax.dot_general(basis, errors, (((1,), (0,)), ((), ())), precision=HI)
    for perm in (CORE, XIN, XOUT):
        right = right + send(right, perm)
    right = right / 8

    grad = lax.dot_general(gathered, output_grads, (((0,), (0,)), ((), ())), preferred_element_type=jnp.float32)
    update = lax.dot_general(basis, right, (((0,), (0,)), ((), ())), precision=HI)
    return ((errors + grad - update)[None], basis.T, right.T)


def solution(mesh):
    placed = (
        P(("replica", "shard"), None),
        P("replica", "shard"),
        P("replica", None, "shard"),
        P("shard", None),
    )
    return jax.shard_map(
        local,
        mesh=mesh,
        in_specs=placed,
        out_specs=(P("replica", None, "shard"), P(), P("shard", None)),
        check_vma=False,
    )
```

```python
import functools

import jax
import jax.numpy as jnp
from jax import lax
from jax.experimental import pallas as pl
from jax.experimental.pallas import tpu as pltpu
from jax.sharding import PartitionSpec as P

ALL = ("replica", "shard")
NX, NC, NZ, NY = 4, 2, 4, 4
RANK = 32
UNIT = 256
PART = 2048
WIDTH = 512
STRIP = 512
F32, BF16 = jnp.float32, jnp.bfloat16
NN, NT, TN = (((1,), (0,)), ((), ())), (((1,), (1,)), ((), ())), (((0,), (0,)), ((), ()))


def pairs(move):
    out = []
    for x in range(NX):
        for c in range(NC):
            for z in range(NZ):
                for y in range(NY):
                    a, b, d, e = move(x, c, z, y)
                    out.append((((x * NC + c) * NZ + z) * NY + y, ((a * NC + b) * NZ + d) * NY + e))
    return out


def inner(v):
    return v ^ 1


def outer(v):
    return 3 - v


def on_p(f):
    return pairs(lambda x, c, z, y: (x, c, z, f(y)) if c == 0 else (x, c, f(z), y))


def on_q(f):
    return pairs(lambda x, c, z, y: (x, c, f(z), y) if c == 0 else (x, c, z, f(y)))


def up(v):
    return (v + 1) % 4


def down(v):
    return (v + 3) % 4


PIN, POUT, QIN, QOUT = on_p(inner), on_p(outer), on_q(inner), on_q(outer)
PUP, PDOWN, QUP, QDOWN = on_p(up), on_p(down), on_q(up), on_q(down)
XIN = pairs(lambda x, c, z, y: (inner(x), c, z, y))
XOUT = pairs(lambda x, c, z, y: (outer(x), c, z, y))
CORE = pairs(lambda x, c, z, y: (x, 1 - c, z, y))


def dot(a, b, dims):
    return lax.dot_general(a, b, dims, preferred_element_type=F32)


def split(a):
    hi = a.astype(BF16)
    rest = a - hi.astype(F32)
    mid = rest.astype(BF16)
    return hi, mid, (rest - mid.astype(F32)).astype(BF16)


def fold(a):
    return a[:RANK] + a[RANK : 2 * RANK] + a[2 * RANK :]


def wide_dot(three, b, dims):
    hi, mid, lo = split(b)
    d = dot(three[: 2 * RANK], mid, dims)
    return fold(dot(three, hi, dims)) + (d[:RANK] + d[RANK:]) + dot(three[:RANK], lo, dims)


def kernel_call(
    body, name, grid, in_specs, out_specs, out_shape, scratch=(), prefetch=0, aliases=None, vmem=16, us=3, after=()
):
    first = prefetch + len(in_specs)

    def run(*refs):
        body(*refs[:first], *refs[first + len(after) :])

    call = pl.pallas_call(
        run,
        grid_spec=pltpu.PrefetchScalarGridSpec(
            num_scalar_prefetch=prefetch,
            grid=grid,
            in_specs=in_specs + [pl.BlockSpec(memory_space=pl.ANY)] * len(after),
            out_specs=out_specs,
            scratch_shapes=list(scratch),
        ),
        out_shape=out_shape,
        input_output_aliases=aliases or {},
        compiler_params=pltpu.CompilerParams(vmem_limit_bytes=vmem * 2**20),
        cost_estimate=pl.CostEstimate(flops=0, bytes_accessed=0, transcendentals=0),
        name=name,
    )
    return lambda *args: call(*args, *after)


def shape(*dims, dtype=F32):
    return jax.ShapeDtypeStruct(dims, dtype)


def turn_kernel(acts, unit0, unit1):
    half = PART // 512
    for dst, inside in ((unit0, pl.program_id(0) < half), (unit1, pl.program_id(0) >= half)):

        @pl.when(inside)
        def _(dst=dst):
            dst[...] = acts[...].T


def turn(acts):
    half = PART // 512
    return kernel_call(
        turn_kernel,
        "turn",
        (2 * half,),
        [pl.BlockSpec((UNIT, 512), lambda i: (0, i))],
        [
            pl.BlockSpec((512, UNIT), lambda i: (jnp.minimum(i, half - 1), 0)),
            pl.BlockSpec((512, UNIT), lambda i: (jnp.maximum(i - half, 0), 0)),
        ],
        [shape(PART, UNIT, dtype=BF16)] * 2,
    )(acts)


def line_kernel(*refs):
    for k, ref in enumerate(refs[:4]):
        refs[-1][:, k * UNIT : (k + 1) * UNIT] = ref[...]


def join_line(units, *after):
    return kernel_call(
        line_kernel,
        "line",
        (PART // 512,),
        [pl.BlockSpec((512, UNIT), lambda i: (i, 0))] * 4,
        pl.BlockSpec((512, 4 * UNIT), lambda i: (i, 0)),
        shape(PART, 4 * UNIT, dtype=BF16),
        after=after,
    )(*units)


def arrange_kernel(order, g0, g1, g2, g3, out):
    for k, g in enumerate((g0, g1, g2, g3)):
        out[k * UNIT : (k + 1) * UNIT, :] = g[...]


def arrange(order, grads):
    def block(t):
        return pl.BlockSpec((UNIT, WIDTH), lambda m, o: (o[4 * m + t], 0))

    return kernel_call(
        arrange_kernel,
        "arrange",
        (4,),
        [block(t) for t in range(4)],
        pl.BlockSpec((4 * UNIT, WIDTH), lambda m, o: (m, 0)),
        shape(*grads.shape, dtype=BF16),
        prefetch=1,
    )(order, *([grads] * 4))


def tokens_kernel(order, factor, g0, g1, g2, g3, out, three):
    @pl.when(pl.program_id(0) == 0)
    def _():
        three[...] = jnp.concatenate(split(factor[...]), 0)

    for i, g in enumerate((g0, g1, g2, g3)):
        out[i] = fold(dot(three[...], g[...], NT))


def tokens(order, factor, grads):
    def block(t):
        return pl.BlockSpec((UNIT, WIDTH), lambda m, o: (o[4 * m + t], 0))

    return kernel_call(
        tokens_kernel,
        "tokens",
        (4,),
        [pl.BlockSpec((RANK, WIDTH), lambda m, o: (0, 0))] + [block(t) for t in range(4)],
        pl.BlockSpec((4, RANK, UNIT), lambda m, o: (m, 0, 0)),
        shape(16, RANK, UNIT),
        [pltpu.VMEM((3 * RANK, WIDTH), BF16)],
        prefetch=1,
    )(order, factor, *([grads] * 4))


def errors_left_kernel(order, factor, err, out, three):
    @pl.when(pl.program_id(0) == 0)
    def _():
        three[...] = jnp.concatenate(split(factor[...]), 0)

    out[0] = wide_dot(three[...], err[...], NT)


def errors_left(order, factor, errors, *after):
    return kernel_call(
        errors_left_kernel,
        "errors_left",
        (8,),
        [
            pl.BlockSpec((RANK, WIDTH), lambda m, o: (0, 0)),
            pl.BlockSpec((512, WIDTH), lambda m, o: (o[m], 0)),
        ],
        pl.BlockSpec((1, RANK, 512), lambda m, o: (m, 0, 0)),
        shape(8, RANK, 512),
        [pltpu.VMEM((3 * RANK, WIDTH), BF16)],
        prefetch=1,
        vmem=56,
        us=9,
        after=after,
    )(order, factor, errors)


def left_kernel(order, u, part, acts, out):
    three = jnp.concatenate(split(u[...]), 0)
    out[0] = part[0] + fold(dot(three, acts[...], NN))


def left_terms(order, u, part, acts):
    return kernel_call(
        left_kernel,
        "left_terms",
        (8,),
        [
            pl.BlockSpec((RANK, UNIT), lambda m, o: (0, 0)),
            pl.BlockSpec((1, RANK, 512), lambda m, o: (m, 0, 0)),
            pl.BlockSpec((UNIT, 512), lambda m, o: (0, o[m])),
        ],
        pl.BlockSpec((1, RANK, 512), lambda m, o: (m, 0, 0)),
        shape(8, RANK, 512),
        prefetch=1,
    )(order, u, part, acts)


def basis_kernel(order, left, basis, six, inv, work):
    gram = None
    for k in range(8):
        g = lax.dot_general(left[k], left[k], NT, precision=lax.Precision.HIGHEST, preferred_element_type=F32)
        gram = g if gram is None else gram + g
    rows = lax.broadcasted_iota(jnp.int32, (RANK, RANK), 0)
    cols = lax.broadcasted_iota(jnp.int32, (RANK, RANK), 1)
    eye = jnp.where(rows == cols, 1.0, 0.0).astype(F32)
    work[...] = jnp.zeros_like(work)
    work[:, :RANK] = gram
    work[:, RANK : 2 * RANK] = eye
    lane = lax.broadcasted_iota(jnp.int32, (RANK, 128), 1)
    sub = lax.broadcasted_iota(jnp.int32, (RANK, 128), 0)

    a = work[...]
    for j in range(RANK):
        col = jnp.sum(jnp.where(lane == j, a, 0.0), axis=1, keepdims=True)
        row = a[j : j + 1, :]
        pivot = col[j : j + 1, :]
        root = lax.rsqrt(pivot)
        root = root * (1.5 - 0.5 * pivot * root * root)
        scaled = row * root
        factor = jnp.where(sub[:, :1] > j, col * root, 0.0)
        a = jnp.where(sub == j, scaled, a - factor * scaled)
    inverse = a[:, RANK : 2 * RANK]
    inv[...] = inverse
    for k in range(8):
        b = lax.dot_general(inverse, left[k], NN, precision=lax.Precision.HIGHEST, preferred_element_type=F32)
        hi, mid, lo = split(b)
        at = pl.ds(pl.multiple_of(order[k] * 512, 512), 512)
        basis[:, at] = b
        six[at, :] = jnp.concatenate([hi, mid, lo, hi, hi, mid], 0).T


def make_basis(order, left):
    return kernel_call(
        basis_kernel,
        "basis",
        (1,),
        [pl.BlockSpec((8, RANK, 512), lambda m, o: (0, 0, 0))],
        [pl.BlockSpec((RANK, 4096), lambda m, o: (0, 0)), pl.BlockSpec((4096, 6 * RANK), lambda m, o: (0, 0)), pl.BlockSpec((RANK, RANK), lambda m, o: (0, 0))],
        [shape(RANK, 4096), shape(4096, 6 * RANK, dtype=BF16), shape(RANK, RANK)],
        [pltpu.VMEM((RANK, 128), F32)],
        prefetch=1,
    )(order, left)


def project_kernel(order, left, acts, out, total):
    m = pl.program_id(0)
    d = dot(jnp.concatenate(split(left[0]), 0), acts[...], NT)

    @pl.when(m == 0)
    def _():
        total[...] = d

    @pl.when(m > 0)
    def _():
        total[...] += d

    out[...] = fold(total[...])


def project(order, left, acts, *after):
    return kernel_call(
        project_kernel,
        "project",
        (8,),
        [pl.BlockSpec((1, RANK, 512), lambda m, o: (m, 0, 0)), pl.BlockSpec((UNIT, 512), lambda m, o: (0, o[m]))],
        pl.BlockSpec((RANK, UNIT), lambda m, o: (0, 0)),
        shape(RANK, UNIT),
        [pltpu.VMEM((3 * RANK, UNIT), F32)],
        prefetch=1,
        after=after,
    )(order, left, acts)


def errors_right_kernel(order, left, err, out):
    d = wide_dot(jnp.concatenate(split(left[0]), 0), err[...], NN)

    @pl.when(pl.program_id(0) == 0)
    def _():
        out[...] = d

    @pl.when(pl.program_id(0) > 0)
    def _():
        out[...] += d


def errors_right(order, left, errors):
    return kernel_call(
        errors_right_kernel,
        "errors_right",
        (8,),
        [pl.BlockSpec((1, RANK, 512), lambda m, o: (m, 0, 0)), pl.BlockSpec((512, WIDTH), lambda m, o: (o[m], 0))],
        pl.BlockSpec((RANK, WIDTH), lambda m, o: (0, 0)),
        shape(RANK, WIDTH),
        prefetch=1,
    )(order, left, errors)


def right_kernel(order, w, part, inverse, g0, g1, g2, g3, out, total):
    m = pl.program_id(0)
    three = jnp.concatenate([jnp.concatenate(v, 0) for v in (split(w[i]) for i in range(4))], 1)
    d = fold(dot(three, jnp.concatenate([g0[...], g1[...], g2[...], g3[...]], 0), NN))

    @pl.when(m == 0)
    def _():
        total[...] = part[...] + d

    @pl.when(m > 0)
    def _():
        total[...] += d

    @pl.when(m == 3)
    def _():
        out[...] = (
            lax.dot_general(
                inverse[...], total[...], NN, precision=lax.Precision.HIGHEST, preferred_element_type=F32
            )
            / 8.0
        )


def right_terms(order, w, part, inverse, grads, *after):
    def block(t):
        return pl.BlockSpec((UNIT, WIDTH), lambda m, o: (o[4 * m + t], 0))

    return kernel_call(
        right_kernel,
        "right_terms",
        (4,),
        [
            pl.BlockSpec((4, RANK, UNIT), lambda m, o: (m, 0, 0)),
            pl.BlockSpec((RANK, WIDTH), lambda m, o: (0, 0)),
            pl.BlockSpec((RANK, RANK), lambda m, o: (0, 0)),
        ]
        + [block(t) for t in range(4)],
        pl.BlockSpec((RANK, WIDTH), lambda m, o: (0, 0)),
        shape(RANK, WIDTH),
        [pltpu.VMEM((RANK, WIDTH), F32)],
        prefetch=1,
        us=40,
        after=after,
    )(order, w, part, inverse, *([grads] * 4))


def rows_kernel(count, updated, base, *refs):
    out = refs[-1]
    total = base[...]
    for x, g in zip(refs[:count], refs[count : 2 * count]):
        total = total + dot(x[...], g[...], NN)
    if updated:
        six, right = refs[2 * count : 2 * count + 2]
        hi, mid, lo = split(right[...])
        total = total - dot(six[...], jnp.concatenate([hi, hi, hi, mid, lo, mid], 0), NN)
    out[...] = total


def add_rows(base, first, pieces, grads, start, of, update=None, buffer=None):
    count = len(pieces)
    depth = pieces[0][0].shape[1]
    write = start // STRIP
    args = [base] + [x for x, _ in pieces] + [grads] * count
    specs = [pl.BlockSpec((STRIP, WIDTH), lambda i: (first + i, 0))]
    specs += [pl.BlockSpec((STRIP, depth), lambda i: (i, 0))] * count
    specs += [pl.BlockSpec((depth, WIDTH), lambda i, t=t: (t, 0)) for _, t in pieces]
    if update is not None:
        args += update
        specs += [
            pl.BlockSpec((STRIP, 6 * RANK), lambda i: (write + i, 0)),
            pl.BlockSpec((RANK, WIDTH), lambda i: (0, 0)),
        ]
    aliases = None
    if buffer is not None:
        aliases = {len(args): 0}
        args.append(buffer)
        specs.append(pl.BlockSpec(memory_space=pl.ANY))
    return kernel_call(
        functools.partial(rows_kernel, count, update is not None),
        "add_rows",
        (PART // STRIP,),
        specs,
        pl.BlockSpec((STRIP, WIDTH), lambda i: (write + i, 0)),
        shape(of, WIDTH),
        aliases=aliases,
        vmem=36,
    )(*args)


def tie_kernel(*refs):
    pass


def tie(a, *after):
    anywhere = pl.BlockSpec(memory_space=pl.ANY)
    return pl.pallas_call(
        tie_kernel,
        in_specs=[anywhere] * (1 + len(after)),
        out_specs=anywhere,
        out_shape=jax.ShapeDtypeStruct(a.shape, a.dtype),
        input_output_aliases={0: 0},
        name="tie",
    )(a, *after)


def pair_kernel(a, b, *rest):
    n = a.shape[0]
    rest[-1][:n] = a[...]
    rest[-1][n:] = b[...]


def pair(a, b, *others):
    return pl.pallas_call(
        pair_kernel,
        out_shape=jax.ShapeDtypeStruct((2 * a.shape[0],) + a.shape[1:], a.dtype),
        compiler_params=pltpu.CompilerParams(vmem_limit_bytes=16 * 2**20),
        name="pair",
    )(a, b, *others)


def send(a, perm):
    return lax.ppermute(a, ALL, perm)


def local(activations, output_grads, error_buffer, previous_factor):
    errors = error_buffer[0]
    rep, sh = lax.axis_index("replica"), lax.axis_index("shard")
    x, core = rep // 2, rep % 2
    z, y = sh // 4, sh % 4
    p = jnp.where(core == 0, y, z)
    q = jnp.where(core == 0, z, y)
    def shard_of(a, b):
        return jnp.where(core == 0, b * 4 + a, a * 4 + b)

    def int_array(v):
        return jnp.stack(v).astype(jnp.int32)

    def codes(v):
        return [v, v ^ 1, 3 - v, (3 - v) ^ 1]

    def ring(v):
        return [v, (v + 3) % 4, (v + 1) % 4, (v + 2) % 4]

    by_code_q = int_array([shard_of(a, b) for b in codes(q) for a in codes(p)])
    by_code = int_array([shard_of(a, b) for a in codes(p) for b in codes(q)])
    by_ring = int_array([shard_of(a, b) for b in ring(q) for a in ring(p)])
    by_rep = int_array([v * 2 + c for c in (core, 1 - core) for b in (x, 3 - x) for v in (b, b ^ 1)])

    def cat(*a, axis=0):
        return jnp.concatenate(a, axis)

    def place(v, origin):
        d = (v - origin) % 4
        return jnp.where(d == 0, 0, jnp.where(d == 3, 1, d + 1))

    in_kept = int_array([4 * place(b, q) + place(a, p) for a in codes(p) for b in codes(q)])
    factor = previous_factor.T
    units = turn(activations)
    above0, below0 = send(units[0], PUP), send(units[0], PDOWN)
    far0, below1 = send(above0, PUP), send(units[1], PDOWN)
    above1, far1 = send(units[1], PUP), send(below1, PDOWN)

    u = tokens(by_code_q, factor, output_grads)
    u = u[:8] + send(u[8:], QOUT)
    u = u[:4] + send(u[4:], QIN)
    u = send(u, CORE)
    u = u[:2] + send(u[2:], QOUT)
    u = u[0] + send(u[1], QIN)
    line0 = join_line((units[0], above0, below0, far0), u)
    top0, bottom0 = send(line0, QUP), send(line0, QDOWN)
    u = send(u, CORE)
    part = errors_left(by_rep, factor, errors, far0)
    left = left_terms(by_rep, u, part, activations)
    left = left[:4] + send(left[4:], CORE)
    left = left[:2] + send(left[2:], XOUT)
    left = left[0] + send(left[1], XIN)
    line1 = join_line((units[1], above1, below1, far1), left)
    top1, bottom1 = send(line1, QUP), send(line1, QDOWN)
    left = left + send(left, PIN)
    left = left + send(left, POUT)
    left = send(left, CORE)
    top0 = tie(top0, left)
    opposite0 = send(top0, QUP)
    left = left + send(left, PIN)
    left = left + send(left, POUT)
    left = left[None]
    left = cat(left, send(left, XIN))
    left = cat(left, send(left, XOUT))
    left = cat(send(left, CORE), left)

    basis, six, inverse = make_basis(by_rep, left)
    part = errors_right(by_rep, left, errors)
    kept = arrange(by_ring, output_grads)
    w = project(by_rep, left, activations, top0, bottom0)[None]
    w = send(w, CORE)
    w = cat(w, send(w, PIN))
    w = pair(w, send(w, POUT), inverse)
    w = send(w, CORE)
    bottom1 = tie(bottom1, w)
    opposite1 = send(bottom1, QDOWN)
    w = pair(w, send(w, PIN), part)
    w = cat(w, send(w, POUT))
    right = right_terms(in_kept, w, part, inverse, kept, opposite0, bottom1)
    for perm in (CORE, XIN, XOUT):
        right = right + send(right, perm)
    update = (six, right)
    sum1 = add_rows(errors, PART // STRIP, ((line1, 0), (bottom1, 2)), kept, 0, PART)
    blocks = ((line0, 0), (top0, 1), (bottom0, 2), (opposite0, 3))
    out = add_rows(errors, 0, blocks, kept, 0, 2 * PART, update)
    out = add_rows(sum1, 0, ((top1, 1), (opposite1, 3)), kept, PART, 2 * PART, update, out)
    return (out[None], basis.T, right.T)


def solution(mesh):
    placed = (
        P(("replica", "shard"), None),
        P("replica", "shard"),
        P("replica", None, "shard"),
        P("shard", None),
    )
    return jax.shard_map(
        local,
        mesh=mesh,
        in_specs=placed,
        out_specs=(P("replica", None, "shard"), P(), P("shard", None)),
        check_vma=False,
    )
```

```python
import functools

import jax
import jax.numpy as jnp
from jax import lax
from jax.experimental import pallas as pl
from jax.experimental.pallas import tpu as pltpu
from jax.sharding import PartitionSpec as P

ALL = ("replica", "shard")
NX, NC, NZ, NY = 4, 2, 4, 4
RANK = 32
UNIT = 256
PART = 2048
WIDTH = 512
STRIP = 512
F32, BF16 = jnp.float32, jnp.bfloat16
NN, NT, TN = (((1,), (0,)), ((), ())), (((1,), (1,)), ((), ())), (((0,), (0,)), ((), ()))


def pairs(move):
    out = []
    for x in range(NX):
        for c in range(NC):
            for z in range(NZ):
                for y in range(NY):
                    a, b, d, e = move(x, c, z, y)
                    out.append((((x * NC + c) * NZ + z) * NY + y, ((a * NC + b) * NZ + d) * NY + e))
    return out


def inner(v):
    return v ^ 1


def outer(v):
    return 3 - v


def on_p(f):
    return pairs(lambda x, c, z, y: (x, c, z, f(y)) if c == 0 else (x, c, f(z), y))


def on_q(f):
    return pairs(lambda x, c, z, y: (x, c, f(z), y) if c == 0 else (x, c, z, f(y)))


def up(v):
    return (v + 1) % 4


def down(v):
    return (v + 3) % 4


PIN, POUT, QIN, QOUT = on_p(inner), on_p(outer), on_q(inner), on_q(outer)
PUP, PDOWN, QUP, QDOWN = on_p(up), on_p(down), on_q(up), on_q(down)
XIN = pairs(lambda x, c, z, y: (inner(x), c, z, y))
XOUT = pairs(lambda x, c, z, y: (outer(x), c, z, y))
CORE = pairs(lambda x, c, z, y: (x, 1 - c, z, y))


def dot(a, b, dims):
    return lax.dot_general(a, b, dims, preferred_element_type=F32)


def split(a):
    hi = a.astype(BF16)
    rest = a - hi.astype(F32)
    mid = rest.astype(BF16)
    return hi, mid, (rest - mid.astype(F32)).astype(BF16)


def fold(a):
    return a[:RANK] + a[RANK : 2 * RANK] + a[2 * RANK :]


def wide_dot(three, b, dims):
    hi, mid, lo = split(b)
    d = dot(three[: 2 * RANK], mid, dims)
    return fold(dot(three, hi, dims)) + (d[:RANK] + d[RANK:]) + dot(three[:RANK], lo, dims)


def kernel_call(
    body, name, grid, in_specs, out_specs, out_shape, scratch=(), prefetch=0, aliases=None, vmem=16, us=3, after=()
):
    first = prefetch + len(in_specs)

    def run(*refs):
        body(*refs[:first], *refs[first + len(after) :])

    call = pl.pallas_call(
        run,
        grid_spec=pltpu.PrefetchScalarGridSpec(
            num_scalar_prefetch=prefetch,
            grid=grid,
            in_specs=in_specs + [pl.BlockSpec(memory_space=pl.ANY)] * len(after),
            out_specs=out_specs,
            scratch_shapes=list(scratch),
        ),
        out_shape=out_shape,
        input_output_aliases=aliases or {},
        compiler_params=pltpu.CompilerParams(vmem_limit_bytes=vmem * 2**20),
        cost_estimate=pl.CostEstimate(flops=0, bytes_accessed=0, transcendentals=0),
        name=name,
    )
    return lambda *args: call(*args, *after)


def shape(*dims, dtype=F32):
    return jax.ShapeDtypeStruct(dims, dtype)


def turn_kernel(acts, out):
    out[...] = acts[...].T


def turn(acts):
    return kernel_call(
        turn_kernel,
        "turn",
        (8,),
        [pl.BlockSpec((UNIT, 512), lambda i: (0, i))],
        pl.BlockSpec((512, UNIT), lambda i: (i, 0)),
        shape(2 * PART, UNIT, dtype=BF16),
    )(acts)


def line_kernel(*refs):
    for k, ref in enumerate(refs[:4]):
        refs[-1][:, k * UNIT : (k + 1) * UNIT] = ref[...]


def join_line(chunk, units, far, *after):
    skip = chunk * (PART // 512)
    return kernel_call(
        line_kernel,
        "line",
        (PART // 512,),
        [pl.BlockSpec((512, UNIT), lambda i: (skip + i, 0))] * 3 + [pl.BlockSpec((512, UNIT), lambda i: (i, 0))],
        pl.BlockSpec((512, 4 * UNIT), lambda i: (i, 0)),
        shape(PART, 4 * UNIT, dtype=BF16),
        after=after,
    )(*units, far)


def arrange_kernel(order, g0, g1, g2, g3, out):
    for k, g in enumerate((g0, g1, g2, g3)):
        out[k * UNIT : (k + 1) * UNIT, :] = g[...]


def arrange(order, grads):
    def block(t):
        return pl.BlockSpec((UNIT, WIDTH), lambda m, o: (o[4 * m + t], 0))

    return kernel_call(
        arrange_kernel,
        "arrange",
        (4,),
        [block(t) for t in range(4)],
        pl.BlockSpec((4 * UNIT, WIDTH), lambda m, o: (m, 0)),
        shape(*grads.shape, dtype=BF16),
        prefetch=1,
    )(order, *([grads] * 4))


def tokens_kernel(order, factor, g0, g1, g2, g3, out, three):
    @pl.when(pl.program_id(0) == 0)
    def _():
        three[...] = jnp.concatenate(split(factor[...]), 0)

    for i, g in enumerate((g0, g1, g2, g3)):
        out[i] = fold(dot(three[...], g[...], NT))


def tokens(order, factor, grads):
    def block(t):
        return pl.BlockSpec((UNIT, WIDTH), lambda m, o: (o[4 * m + t], 0))

    return kernel_call(
        tokens_kernel,
        "tokens",
        (4,),
        [pl.BlockSpec((RANK, WIDTH), lambda m, o: (0, 0))] + [block(t) for t in range(4)],
        pl.BlockSpec((4, RANK, UNIT), lambda m, o: (m, 0, 0)),
        shape(16, RANK, UNIT),
        [pltpu.VMEM((3 * RANK, WIDTH), BF16)],
        prefetch=1,
    )(order, factor, *([grads] * 4))


def errors_left_kernel(order, factor, err, out, three):
    @pl.when(pl.program_id(0) == 0)
    def _():
        three[...] = jnp.concatenate(split(factor[...]), 0)

    out[0] = wide_dot(three[...], err[...], NT)


def errors_left(order, factor, errors, *after):
    return kernel_call(
        errors_left_kernel,
        "errors_left",
        (8,),
        [
            pl.BlockSpec((RANK, WIDTH), lambda m, o: (0, 0)),
            pl.BlockSpec((512, WIDTH), lambda m, o: (o[m], 0)),
        ],
        pl.BlockSpec((1, RANK, 512), lambda m, o: (m, 0, 0)),
        shape(8, RANK, 512),
        [pltpu.VMEM((3 * RANK, WIDTH), BF16)],
        prefetch=1,
        vmem=56,
        us=9,
        after=after,
    )(order, factor, errors)


def left_kernel(order, u, part, acts, out):
    three = jnp.concatenate(split(u[...]), 0)
    out[0] = part[0] + fold(dot(three, acts[...], NN))


def left_terms(order, u, part, acts, *after):
    return kernel_call(
        left_kernel,
        "left_terms",
        (8,),
        [
            pl.BlockSpec((RANK, UNIT), lambda m, o: (0, 0)),
            pl.BlockSpec((1, RANK, 512), lambda m, o: (m, 0, 0)),
            pl.BlockSpec((UNIT, 512), lambda m, o: (0, o[m])),
        ],
        pl.BlockSpec((1, RANK, 512), lambda m, o: (m, 0, 0)),
        shape(8, RANK, 512),
        prefetch=1,
        after=after,
    )(order, u, part, acts)


def basis_kernel(order, left, basis, six, inv, work):
    gram = None
    for k in range(8):
        g = lax.dot_general(left[k], left[k], NT, precision=lax.Precision.HIGHEST, preferred_element_type=F32)
        gram = g if gram is None else gram + g
    rows = lax.broadcasted_iota(jnp.int32, (RANK, RANK), 0)
    cols = lax.broadcasted_iota(jnp.int32, (RANK, RANK), 1)
    eye = jnp.where(rows == cols, 1.0, 0.0).astype(F32)
    work[...] = jnp.zeros_like(work)
    work[:, :RANK] = gram
    work[:, RANK : 2 * RANK] = eye
    lane = lax.broadcasted_iota(jnp.int32, (RANK, 128), 1)
    sub = lax.broadcasted_iota(jnp.int32, (RANK, 128), 0)

    a = work[...]
    for j in range(RANK):
        col = jnp.sum(jnp.where(lane == j, a, 0.0), axis=1, keepdims=True)
        row = a[j : j + 1, :]
        pivot = col[j : j + 1, :]
        root = lax.rsqrt(pivot)
        root = root * (1.5 - 0.5 * pivot * root * root)
        scaled = row * root
        factor = jnp.where(sub[:, :1] > j, col * root, 0.0)
        a = jnp.where(sub == j, scaled, a - factor * scaled)
    inverse = a[:, RANK : 2 * RANK]
    inv[...] = inverse
    for k in range(8):
        b = lax.dot_general(inverse, left[k], NN, precision=lax.Precision.HIGHEST, preferred_element_type=F32)
        hi, mid, lo = split(b)
        at = pl.ds(pl.multiple_of(order[k] * 512, 512), 512)
        basis[:, at] = b
        six[at, :] = jnp.concatenate([hi, mid, lo, hi, hi, mid], 0).T


def make_basis(order, left):
    return kernel_call(
        basis_kernel,
        "basis",
        (1,),
        [pl.BlockSpec((8, RANK, 512), lambda m, o: (0, 0, 0))],
        [pl.BlockSpec((RANK, 4096), lambda m, o: (0, 0)), pl.BlockSpec((4096, 6 * RANK), lambda m, o: (0, 0)), pl.BlockSpec((RANK, RANK), lambda m, o: (0, 0))],
        [shape(RANK, 4096), shape(4096, 6 * RANK, dtype=BF16), shape(RANK, RANK)],
        [pltpu.VMEM((RANK, 128), F32)],
        prefetch=1,
    )(order, left)


def project_kernel(order, left, acts, out, total):
    m = pl.program_id(0)
    d = dot(jnp.concatenate(split(left[0]), 0), acts[...], NT)

    @pl.when(m == 0)
    def _():
        total[...] = d

    @pl.when(m > 0)
    def _():
        total[...] += d

    out[...] = fold(total[...])


def project(order, left, acts, *after):
    return kernel_call(
        project_kernel,
        "project",
        (8,),
        [pl.BlockSpec((1, RANK, 512), lambda m, o: (m, 0, 0)), pl.BlockSpec((UNIT, 512), lambda m, o: (0, o[m]))],
        pl.BlockSpec((RANK, UNIT), lambda m, o: (0, 0)),
        shape(RANK, UNIT),
        [pltpu.VMEM((3 * RANK, UNIT), F32)],
        prefetch=1,
        after=after,
    )(order, left, acts)


def errors_right_kernel(order, left, err, out):
    d = wide_dot(jnp.concatenate(split(left[0]), 0), err[...], NN)

    @pl.when(pl.program_id(0) == 0)
    def _():
        out[...] = d

    @pl.when(pl.program_id(0) > 0)
    def _():
        out[...] += d


def errors_right(order, left, errors):
    return kernel_call(
        errors_right_kernel,
        "errors_right",
        (8,),
        [pl.BlockSpec((1, RANK, 512), lambda m, o: (m, 0, 0)), pl.BlockSpec((512, WIDTH), lambda m, o: (o[m], 0))],
        pl.BlockSpec((RANK, WIDTH), lambda m, o: (0, 0)),
        shape(RANK, WIDTH),
        prefetch=1,
    )(order, left, errors)


def right_kernel(order, w, part, inverse, g0, g1, g2, g3, out, total):
    m = pl.program_id(0)
    three = jnp.concatenate([jnp.concatenate(v, 0) for v in (split(w[i]) for i in range(4))], 1)
    d = fold(dot(three, jnp.concatenate([g0[...], g1[...], g2[...], g3[...]], 0), NN))

    @pl.when(m == 0)
    def _():
        total[...] = part[...] + d

    @pl.when(m > 0)
    def _():
        total[...] += d

    @pl.when(m == 3)
    def _():
        out[...] = (
            lax.dot_general(
                inverse[...], total[...], NN, precision=lax.Precision.HIGHEST, preferred_element_type=F32
            )
            / 8.0
        )


def right_terms(order, w, part, inverse, grads, *after):
    def block(t):
        return pl.BlockSpec((UNIT, WIDTH), lambda m, o: (o[4 * m + t], 0))

    return kernel_call(
        right_kernel,
        "right_terms",
        (4,),
        [
            pl.BlockSpec((4, RANK, UNIT), lambda m, o: (m, 0, 0)),
            pl.BlockSpec((RANK, WIDTH), lambda m, o: (0, 0)),
            pl.BlockSpec((RANK, RANK), lambda m, o: (0, 0)),
        ]
        + [block(t) for t in range(4)],
        pl.BlockSpec((RANK, WIDTH), lambda m, o: (0, 0)),
        shape(RANK, WIDTH),
        [pltpu.VMEM((RANK, WIDTH), F32)],
        prefetch=1,
        us=40,
        after=after,
    )(order, w, part, inverse, *([grads] * 4))


def rows_kernel(count, updated, base, *refs):
    out = refs[-1]
    total = base[...]
    for x, g in zip(refs[:count], refs[count : 2 * count]):
        total = total + dot(x[...], g[...], NN)
    if updated:
        six, right = refs[2 * count : 2 * count + 2]
        hi, mid, lo = split(right[...])
        total = total - dot(six[...], jnp.concatenate([hi, hi, hi, mid, lo, mid], 0), NN)
    out[...] = total


def add_rows(base, first, pieces, grads, start, of, update=None, buffer=None):
    count = len(pieces)
    depth = pieces[0][0].shape[1]
    write = start // STRIP
    args = [base] + [x for x, _ in pieces] + [grads] * count
    specs = [pl.BlockSpec((STRIP, WIDTH), lambda i: (first + i, 0))]
    specs += [pl.BlockSpec((STRIP, depth), lambda i: (i, 0))] * count
    specs += [pl.BlockSpec((depth, WIDTH), lambda i, t=t: (t, 0)) for _, t in pieces]
    if update is not None:
        args += update
        specs += [
            pl.BlockSpec((STRIP, 6 * RANK), lambda i: (write + i, 0)),
            pl.BlockSpec((RANK, WIDTH), lambda i: (0, 0)),
        ]
    aliases = None
    if buffer is not None:
        aliases = {len(args): 0}
        args.append(buffer)
        specs.append(pl.BlockSpec(memory_space=pl.ANY))
    return kernel_call(
        functools.partial(rows_kernel, count, update is not None),
        "add_rows",
        (PART // STRIP,),
        specs,
        pl.BlockSpec((STRIP, WIDTH), lambda i: (write + i, 0)),
        shape(of, WIDTH),
        aliases=aliases,
        vmem=36,
    )(*args)


def tie_kernel(*refs):
    pass


def tie(a, *after):
    anywhere = pl.BlockSpec(memory_space=pl.ANY)
    return pl.pallas_call(
        tie_kernel,
        in_specs=[anywhere] * (1 + len(after)),
        out_specs=anywhere,
        out_shape=jax.ShapeDtypeStruct(a.shape, a.dtype),
        input_output_aliases={0: 0},
        name="tie",
    )(a, *after)


def halve_kernel(u, r, *rest):
    rest[-1][...] = u[: r.shape[0]] + r[...]


def halve(u, r, *after):
    vmem = pl.BlockSpec(memory_space=pltpu.VMEM)
    return pl.pallas_call(
        halve_kernel,
        in_specs=[vmem] * 2 + [pl.BlockSpec(memory_space=pl.ANY)] * len(after),
        out_specs=vmem,
        out_shape=jax.ShapeDtypeStruct(r.shape, r.dtype),
        compiler_params=pltpu.CompilerParams(vmem_limit_bytes=16 * 2**20),
        name="halve",
    )(u, r, *after)


def pair_kernel(a, b, *rest):
    n = a.shape[0]
    rest[-1][:n] = a[...]
    rest[-1][n:] = b[...]


def pair(a, b, *others):
    vmem = pl.BlockSpec(memory_space=pltpu.VMEM)
    return pl.pallas_call(
        pair_kernel,
        in_specs=[vmem] * 2 + [pl.BlockSpec(memory_space=pl.ANY)] * len(others),
        out_specs=vmem,
        out_shape=jax.ShapeDtypeStruct((2 * a.shape[0],) + a.shape[1:], a.dtype),
        compiler_params=pltpu.CompilerParams(vmem_limit_bytes=16 * 2**20),
        name="pair",
    )(a, b, *others)


def send(a, perm):
    return lax.ppermute(a, ALL, perm)


def local(activations, output_grads, error_buffer, previous_factor):
    errors = error_buffer[0]
    rep, sh = lax.axis_index("replica"), lax.axis_index("shard")
    x, core = rep // 2, rep % 2
    z, y = sh // 4, sh % 4
    p = jnp.where(core == 0, y, z)
    q = jnp.where(core == 0, z, y)
    def shard_of(a, b):
        return jnp.where(core == 0, b * 4 + a, a * 4 + b)

    def int_array(v):
        return jnp.stack(v).astype(jnp.int32)

    def codes(v):
        return [v, v ^ 1, 3 - v, (3 - v) ^ 1]

    def ring(v):
        return [v, (v + 3) % 4, (v + 1) % 4, (v + 2) % 4]

    by_code_q = int_array([shard_of(a, b) for b in codes(q) for a in codes(p)])
    by_code = int_array([shard_of(a, b) for a in codes(p) for b in codes(q)])
    by_ring = int_array([shard_of(a, b) for b in ring(q) for a in ring(p)])
    by_rep = int_array([v * 2 + c for c in (core, 1 - core) for b in (x, 3 - x) for v in (b, b ^ 1)])

    def cat(*a, axis=0):
        return jnp.concatenate(a, axis)

    def place(v, origin):
        d = (v - origin) % 4
        return jnp.where(d == 0, 0, jnp.where(d == 3, 1, d + 1))

    in_kept = int_array([4 * place(b, q) + place(a, p) for a in codes(p) for b in codes(q)])
    factor = previous_factor.T
    units = turn(activations)
    above, below = send(units, PUP), send(units, PDOWN)
    far0, far1 = send(above[:PART], PUP), send(below[PART:], PDOWN)
    units = (units, above, below)

    u = tokens(by_code_q, factor, output_grads)
    part = errors_left(by_rep, factor, errors)
    u = halve(u, send(u[8:], QOUT), part)
    u = u[:4] + send(u[4:], QIN)
    u = send(u, CORE)
    u = u[:2] + send(u[2:], QOUT)
    u = u[0] + send(u[1], QIN)
    line0 = join_line(0, units, far0, u, far1)
    top0, bottom0 = send(line0, QUP), send(line0, QDOWN)
    u = send(u, CORE)
    left = left_terms(by_rep, u, part, activations, line0)
    left = left[:4] + send(left[4:], CORE)
    left = left[:2] + send(left[2:], XOUT)
    line1 = join_line(1, units, far1, left)
    top1, bottom1 = send(line1, QUP), send(line1, QDOWN)
    left = halve(left, send(left[1:], XIN), line1)[0]
    left = left + send(left, PIN)
    left = left + send(left, POUT)
    left = send(left, CORE)
    top0 = tie(top0, left, bottom0)
    opposite0 = send(top0, QUP)
    left = left + send(left, PIN)
    left = left + send(left, POUT)
    left = left[None]
    left = cat(left, send(left, XIN))
    left = cat(left, send(left, XOUT))
    left = cat(send(left, CORE), left)

    basis, six, inverse = make_basis(by_rep, left)
    part = errors_right(by_rep, left, errors)
    kept = arrange(by_ring, output_grads)
    w = project(by_rep, left, activations, top0, bottom0)[None]
    w = send(w, CORE)
    w = cat(w, send(w, PIN))
    w = pair(w, send(w, POUT), inverse)
    w = send(w, CORE)
    sum0 = add_rows(errors, 0, ((line0, 0), (top0, 1), (bottom0, 2)), kept, 0, PART)
    bottom1 = tie(bottom1, w, sum0)
    opposite1 = send(bottom1, QDOWN)
    sum1 = add_rows(errors, PART // STRIP, ((line1, 0), (bottom1, 2)), kept, 0, PART)
    w = pair(w, send(w, PIN), part, sum0, sum1, opposite0)
    w = cat(w, send(w, POUT))
    right = right_terms(in_kept, w, part, inverse, kept)
    for perm in (CORE, XIN, XOUT):
        right = right + send(right, perm)
    update = (six, right)
    out = add_rows(sum0, 0, ((opposite0, 3),), kept, 0, 2 * PART, update)
    out = add_rows(sum1, 0, ((top1, 1), (opposite1, 3)), kept, PART, 2 * PART, update, out)
    return (out[None], basis.T, right.T)


def solution(mesh):
    placed = (
        P(("replica", "shard"), None),
        P("replica", "shard"),
        P("replica", None, "shard"),
        P("shard", None),
    )
    return jax.shard_map(
        local,
        mesh=mesh,
        in_specs=placed,
        out_specs=(P("replica", None, "shard"), P(), P("shard", None)),
        check_vma=False,
    )
```

```python
import functools

import jax
import jax.numpy as jnp
from jax import lax
from jax.experimental import pallas as pl
from jax.experimental.pallas import tpu as pltpu
from jax.sharding import PartitionSpec as P

ALL = ("replica", "shard")
NX, NC, NZ, NY = 4, 2, 4, 4
RANK = 32
UNIT = 256
PART = 2048
WIDTH = 512
STRIP = 512
F32, BF16 = jnp.float32, jnp.bfloat16
NN, NT, TN = (((1,), (0,)), ((), ())), (((1,), (1,)), ((), ())), (((0,), (0,)), ((), ()))


def pairs(move):
    out = []
    for x in range(NX):
        for c in range(NC):
            for z in range(NZ):
                for y in range(NY):
                    a, b, d, e = move(x, c, z, y)
                    out.append((((x * NC + c) * NZ + z) * NY + y, ((a * NC + b) * NZ + d) * NY + e))
    return out


def inner(v):
    return v ^ 1


def outer(v):
    return 3 - v


def on_p(f):
    return pairs(lambda x, c, z, y: (x, c, z, f(y)) if c == 0 else (x, c, f(z), y))


def on_q(f):
    return pairs(lambda x, c, z, y: (x, c, f(z), y) if c == 0 else (x, c, z, f(y)))


def up(v):
    return (v + 1) % 4


def down(v):
    return (v + 3) % 4


PIN, POUT, QIN, QOUT = on_p(inner), on_p(outer), on_q(inner), on_q(outer)
PUP, PDOWN, QUP, QDOWN = on_p(up), on_p(down), on_q(up), on_q(down)
XIN = pairs(lambda x, c, z, y: (inner(x), c, z, y))
XOUT = pairs(lambda x, c, z, y: (outer(x), c, z, y))
CORE = pairs(lambda x, c, z, y: (x, 1 - c, z, y))


def dot(a, b, dims):
    return lax.dot_general(a, b, dims, preferred_element_type=F32)


def split(a):
    hi = a.astype(BF16)
    rest = a - hi.astype(F32)
    mid = rest.astype(BF16)
    return hi, mid, (rest - mid.astype(F32)).astype(BF16)


def fold(a):
    return a[:RANK] + a[RANK : 2 * RANK] + a[2 * RANK :]


def wide_dot(three, b, dims):
    hi, mid, lo = split(b)
    d = dot(three[: 2 * RANK], mid, dims)
    return fold(dot(three, hi, dims)) + (d[:RANK] + d[RANK:]) + dot(three[:RANK], lo, dims)


def kernel_call(
    body, name, grid, in_specs, out_specs, out_shape, scratch=(), prefetch=0, aliases=None, vmem=16, us=3, after=()
):
    first = prefetch + len(in_specs)

    def run(*refs):
        body(*refs[:first], *refs[first + len(after) :])

    call = pl.pallas_call(
        run,
        grid_spec=pltpu.PrefetchScalarGridSpec(
            num_scalar_prefetch=prefetch,
            grid=grid,
            in_specs=in_specs + [pl.BlockSpec(memory_space=pl.ANY)] * len(after),
            out_specs=out_specs,
            scratch_shapes=list(scratch),
        ),
        out_shape=out_shape,
        input_output_aliases=aliases or {},
        compiler_params=pltpu.CompilerParams(vmem_limit_bytes=vmem * 2**20),
        cost_estimate=pl.CostEstimate(flops=0, bytes_accessed=0, transcendentals=0),
        name=name,
    )
    return lambda *args: call(*args, *after)


def shape(*dims, dtype=F32):
    return jax.ShapeDtypeStruct(dims, dtype)


def turn_kernel(acts, out):
    out[...] = acts[...].T


def turn(acts):
    return kernel_call(
        turn_kernel,
        "turn",
        (8,),
        [pl.BlockSpec((UNIT, 512), lambda i: (0, i))],
        pl.BlockSpec((512, UNIT), lambda i: (i, 0)),
        shape(2 * PART, UNIT, dtype=BF16),
    )(acts)


def line_kernel(*refs):
    for k, ref in enumerate(refs[:4]):
        refs[-1][:, k * UNIT : (k + 1) * UNIT] = ref[...]


def join_line(chunk, units, far, *after):
    skip = chunk * (PART // 512)
    return kernel_call(
        line_kernel,
        "line",
        (PART // 512,),
        [pl.BlockSpec((512, UNIT), lambda i: (skip + i, 0))] * 3 + [pl.BlockSpec((512, UNIT), lambda i: (i, 0))],
        pl.BlockSpec((512, 4 * UNIT), lambda i: (i, 0)),
        shape(PART, 4 * UNIT, dtype=BF16),
        after=after,
    )(*units, far)


def arrange_kernel(order, g0, g1, g2, g3, out):
    for k, g in enumerate((g0, g1, g2, g3)):
        out[k * UNIT : (k + 1) * UNIT, :] = g[...]


def arrange(order, grads):
    def block(t):
        return pl.BlockSpec((UNIT, WIDTH), lambda m, o: (o[4 * m + t], 0))

    return kernel_call(
        arrange_kernel,
        "arrange",
        (4,),
        [block(t) for t in range(4)],
        pl.BlockSpec((4 * UNIT, WIDTH), lambda m, o: (m, 0)),
        shape(*grads.shape, dtype=BF16),
        prefetch=1,
    )(order, *([grads] * 4))


def tokens_kernel(order, factor, g0, g1, g2, g3, out, three):
    @pl.when(pl.program_id(0) == 0)
    def _():
        three[...] = jnp.concatenate(split(factor[...]), 0)

    for i, g in enumerate((g0, g1, g2, g3)):
        out[i] = fold(dot(three[...], g[...], NT))


def tokens(order, factor, grads):
    def block(t):
        return pl.BlockSpec((UNIT, WIDTH), lambda m, o: (o[4 * m + t], 0))

    return kernel_call(
        tokens_kernel,
        "tokens",
        (4,),
        [pl.BlockSpec((RANK, WIDTH), lambda m, o: (0, 0))] + [block(t) for t in range(4)],
        pl.BlockSpec((4, RANK, UNIT), lambda m, o: (m, 0, 0)),
        shape(16, RANK, UNIT),
        [pltpu.VMEM((3 * RANK, WIDTH), BF16)],
        prefetch=1,
    )(order, factor, *([grads] * 4))


def errors_left_kernel(order, factor, err, out, three):
    @pl.when(pl.program_id(0) == 0)
    def _():
        three[...] = jnp.concatenate(split(factor[...]), 0)

    out[0] = wide_dot(three[...], err[...], NT)


def errors_left(order, factor, errors, *after):
    return kernel_call(
        errors_left_kernel,
        "errors_left",
        (8,),
        [
            pl.BlockSpec((RANK, WIDTH), lambda m, o: (0, 0)),
            pl.BlockSpec((512, WIDTH), lambda m, o: (o[m], 0)),
        ],
        pl.BlockSpec((1, RANK, 512), lambda m, o: (m, 0, 0)),
        shape(8, RANK, 512),
        [pltpu.VMEM((3 * RANK, WIDTH), BF16)],
        prefetch=1,
        vmem=56,
        us=9,
        after=after,
    )(order, factor, errors)


def left_kernel(order, u, part, acts, out):
    three = jnp.concatenate(split(u[...]), 0)
    out[0] = part[0] + fold(dot(three, acts[...], NN))


def left_terms(order, u, part, acts, *after):
    return kernel_call(
        left_kernel,
        "left_terms",
        (8,),
        [
            pl.BlockSpec((RANK, UNIT), lambda m, o: (0, 0)),
            pl.BlockSpec((1, RANK, 512), lambda m, o: (m, 0, 0)),
            pl.BlockSpec((UNIT, 512), lambda m, o: (0, o[m])),
        ],
        pl.BlockSpec((1, RANK, 512), lambda m, o: (m, 0, 0)),
        shape(8, RANK, 512),
        prefetch=1,
        after=after,
    )(order, u, part, acts)


def basis_kernel(order, left, basis, six, inv, work):
    gram = None
    for k in range(8):
        g = lax.dot_general(left[k], left[k], NT, precision=lax.Precision.HIGHEST, preferred_element_type=F32)
        gram = g if gram is None else gram + g
    rows = lax.broadcasted_iota(jnp.int32, (RANK, RANK), 0)
    cols = lax.broadcasted_iota(jnp.int32, (RANK, RANK), 1)
    eye = jnp.where(rows == cols, 1.0, 0.0).astype(F32)
    work[...] = jnp.zeros_like(work)
    work[:, :RANK] = gram
    work[:, RANK : 2 * RANK] = eye
    lane = lax.broadcasted_iota(jnp.int32, (RANK, 128), 1)
    sub = lax.broadcasted_iota(jnp.int32, (RANK, 128), 0)

    a = work[...]
    for j in range(RANK):
        col = jnp.sum(jnp.where(lane == j, a, 0.0), axis=1, keepdims=True)
        row = a[j : j + 1, :]
        pivot = col[j : j + 1, :]
        root = lax.rsqrt(pivot)
        root = root * (1.5 - 0.5 * pivot * root * root)
        scaled = row * root
        factor = jnp.where(sub[:, :1] > j, col * root, 0.0)
        a = jnp.where(sub == j, scaled, a - factor * scaled)
    inverse = a[:, RANK : 2 * RANK]
    inv[...] = inverse
    for k in range(8):
        b = lax.dot_general(inverse, left[k], NN, precision=lax.Precision.HIGHEST, preferred_element_type=F32)
        hi, mid, lo = split(b)
        at = pl.ds(pl.multiple_of(order[k] * 512, 512), 512)
        basis[:, at] = b
        six[at, :] = jnp.concatenate([hi, mid, lo, hi, hi, mid], 0).T


def make_basis(order, left):
    return kernel_call(
        basis_kernel,
        "basis",
        (1,),
        [pl.BlockSpec((8, RANK, 512), lambda m, o: (0, 0, 0))],
        [pl.BlockSpec((RANK, 4096), lambda m, o: (0, 0)), pl.BlockSpec((4096, 6 * RANK), lambda m, o: (0, 0)), pl.BlockSpec((RANK, RANK), lambda m, o: (0, 0))],
        [shape(RANK, 4096), shape(4096, 6 * RANK, dtype=BF16), shape(RANK, RANK)],
        [pltpu.VMEM((RANK, 128), F32)],
        prefetch=1,
    )(order, left)


def project_kernel(order, left, acts, out, total):
    m = pl.program_id(0)
    d = dot(jnp.concatenate(split(left[0]), 0), acts[...], NT)

    @pl.when(m == 0)
    def _():
        total[...] = d

    @pl.when(m > 0)
    def _():
        total[...] += d

    out[...] = fold(total[...])


def project(order, left, acts, *after):
    return kernel_call(
        project_kernel,
        "project",
        (8,),
        [pl.BlockSpec((1, RANK, 512), lambda m, o: (m, 0, 0)), pl.BlockSpec((UNIT, 512), lambda m, o: (0, o[m]))],
        pl.BlockSpec((RANK, UNIT), lambda m, o: (0, 0)),
        shape(RANK, UNIT),
        [pltpu.VMEM((3 * RANK, UNIT), F32)],
        prefetch=1,
        after=after,
    )(order, left, acts)


def errors_right_kernel(order, left, err, out):
    d = wide_dot(jnp.concatenate(split(left[0]), 0), err[...], NN)

    @pl.when(pl.program_id(0) == 0)
    def _():
        out[...] = d

    @pl.when(pl.program_id(0) > 0)
    def _():
        out[...] += d


def errors_right(order, left, errors):
    return kernel_call(
        errors_right_kernel,
        "errors_right",
        (8,),
        [pl.BlockSpec((1, RANK, 512), lambda m, o: (m, 0, 0)), pl.BlockSpec((512, WIDTH), lambda m, o: (o[m], 0))],
        pl.BlockSpec((RANK, WIDTH), lambda m, o: (0, 0)),
        shape(RANK, WIDTH),
        prefetch=1,
    )(order, left, errors)


def right_kernel(order, w, part, inverse, g0, g1, g2, g3, out, total):
    m = pl.program_id(0)
    three = jnp.concatenate([jnp.concatenate(v, 0) for v in (split(w[i]) for i in range(4))], 1)
    d = fold(dot(three, jnp.concatenate([g0[...], g1[...], g2[...], g3[...]], 0), NN))

    @pl.when(m == 0)
    def _():
        total[...] = part[...] + d

    @pl.when(m > 0)
    def _():
        total[...] += d

    @pl.when(m == 3)
    def _():
        out[...] = (
            lax.dot_general(
                inverse[...], total[...], NN, precision=lax.Precision.HIGHEST, preferred_element_type=F32
            )
            / 8.0
        )


def right_terms(order, w, part, inverse, grads, *after):
    def block(t):
        return pl.BlockSpec((UNIT, WIDTH), lambda m, o: (o[4 * m + t], 0))

    return kernel_call(
        right_kernel,
        "right_terms",
        (4,),
        [
            pl.BlockSpec((4, RANK, UNIT), lambda m, o: (m, 0, 0)),
            pl.BlockSpec((RANK, WIDTH), lambda m, o: (0, 0)),
            pl.BlockSpec((RANK, RANK), lambda m, o: (0, 0)),
        ]
        + [block(t) for t in range(4)],
        pl.BlockSpec((RANK, WIDTH), lambda m, o: (0, 0)),
        shape(RANK, WIDTH),
        [pltpu.VMEM((RANK, WIDTH), F32)],
        prefetch=1,
        us=40,
        after=after,
    )(order, w, part, inverse, *([grads] * 4))


def rows_kernel(count, updated, base, *refs):
    out = refs[-1]
    total = base[...]
    for x, g in zip(refs[:count], refs[count : 2 * count]):
        total = total + dot(x[...], g[...], NN)
    if updated:
        six, right = refs[2 * count : 2 * count + 2]
        hi, mid, lo = split(right[...])
        total = total - dot(six[...], jnp.concatenate([hi, hi, hi, mid, lo, mid], 0), NN)
    out[...] = total


def add_rows(base, first, pieces, grads, start, of, update=None, buffer=None):
    count = len(pieces)
    depth = pieces[0][0].shape[1]
    write = start // STRIP
    args = [base] + [x for x, _ in pieces] + [grads] * count
    specs = [pl.BlockSpec((STRIP, WIDTH), lambda i: (first + i, 0))]
    specs += [pl.BlockSpec((STRIP, depth), lambda i: (i, 0))] * count
    specs += [pl.BlockSpec((depth, WIDTH), lambda i, t=t: (t, 0)) for _, t in pieces]
    if update is not None:
        args += update
        specs += [
            pl.BlockSpec((STRIP, 6 * RANK), lambda i: (write + i, 0)),
            pl.BlockSpec((RANK, WIDTH), lambda i: (0, 0)),
        ]
    aliases = None
    if buffer is not None:
        aliases = {len(args): 0}
        args.append(buffer)
        specs.append(pl.BlockSpec(memory_space=pl.ANY))
    return kernel_call(
        functools.partial(rows_kernel, count, update is not None),
        "add_rows",
        (PART // STRIP,),
        specs,
        pl.BlockSpec((STRIP, WIDTH), lambda i: (write + i, 0)),
        shape(of, WIDTH),
        aliases=aliases,
        vmem=36,
    )(*args)


def tie_kernel(*refs):
    pass


def tie(a, *after):
    anywhere = pl.BlockSpec(memory_space=pl.ANY)
    return pl.pallas_call(
        tie_kernel,
        in_specs=[anywhere] * (1 + len(after)),
        out_specs=anywhere,
        out_shape=jax.ShapeDtypeStruct(a.shape, a.dtype),
        input_output_aliases={0: 0},
        name="tie",
    )(a, *after)


def halve_kernel(u, r, *rest):
    rest[-1][...] = u[: r.shape[0]] + r[...]


def halve(u, r, *after):
    vmem = pl.BlockSpec(memory_space=pltpu.VMEM)
    return pl.pallas_call(
        halve_kernel,
        in_specs=[vmem] * 2 + [pl.BlockSpec(memory_space=pl.ANY)] * len(after),
        out_specs=vmem,
        out_shape=jax.ShapeDtypeStruct(r.shape, r.dtype),
        compiler_params=pltpu.CompilerParams(vmem_limit_bytes=16 * 2**20),
        name="halve",
    )(u, r, *after)


def pair_kernel(a, b, *rest):
    n = a.shape[0]
    rest[-1][:n] = a[...]
    rest[-1][n:] = b[...]


def pair(a, b, *others):
    vmem = pl.BlockSpec(memory_space=pltpu.VMEM)
    return pl.pallas_call(
        pair_kernel,
        in_specs=[vmem] * 2 + [pl.BlockSpec(memory_space=pl.ANY)] * len(others),
        out_specs=vmem,
        out_shape=jax.ShapeDtypeStruct((2 * a.shape[0],) + a.shape[1:], a.dtype),
        compiler_params=pltpu.CompilerParams(vmem_limit_bytes=16 * 2**20),
        name="pair",
    )(a, b, *others)


def send(a, perm):
    return lax.ppermute(a, ALL, perm)


def local(activations, output_grads, error_buffer, previous_factor):
    errors = error_buffer[0]
    rep, sh = lax.axis_index("replica"), lax.axis_index("shard")
    x, core = rep // 2, rep % 2
    z, y = sh // 4, sh % 4
    p = jnp.where(core == 0, y, z)
    q = jnp.where(core == 0, z, y)
    def shard_of(a, b):
        return jnp.where(core == 0, b * 4 + a, a * 4 + b)

    def int_array(v):
        return jnp.stack(v).astype(jnp.int32)

    def codes(v):
        return [v, v ^ 1, 3 - v, (3 - v) ^ 1]

    def ring(v):
        return [v, (v + 3) % 4, (v + 1) % 4, (v + 2) % 4]

    by_code_q = int_array([shard_of(a, b) for b in codes(q) for a in codes(p)])
    by_code = int_array([shard_of(a, b) for a in codes(p) for b in codes(q)])
    by_ring = int_array([shard_of(a, b) for b in ring(q) for a in ring(p)])
    by_rep = int_array([v * 2 + c for c in (core, 1 - core) for b in (x, 3 - x) for v in (b, b ^ 1)])

    def cat(*a, axis=0):
        return jnp.concatenate(a, axis)

    def place(v, origin):
        d = (v - origin) % 4
        return jnp.where(d == 0, 0, jnp.where(d == 3, 1, d + 1))

    in_kept = int_array([4 * place(b, q) + place(a, p) for a in codes(p) for b in codes(q)])
    factor = previous_factor.T
    units = turn(activations)
    above, below = send(units, PUP), send(units, PDOWN)
    far0, far1 = send(above[:PART], PUP), send(below[PART:], PDOWN)
    units = (units, above, below)

    u = tokens(by_code_q, factor, output_grads)
    part = errors_left(by_rep, factor, errors)
    u = halve(u, send(u[8:], QOUT), part)
    u = u[:4] + send(u[4:], QIN)
    u = send(u, CORE)
    u = u[:2] + send(u[2:], QOUT)
    u = u[0] + send(u[1], QIN)
    line0 = join_line(0, units, far0, u, far1)
    top0, bottom0 = send(line0, QUP), send(line0, QDOWN)
    u = send(u, CORE)
    left = left_terms(by_rep, u, part, activations, line0)
    left = left[:4] + send(left[4:], CORE)
    left = left[:2] + send(left[2:], XOUT)
    line1 = join_line(1, units, far1, left)
    top1, bottom1 = send(line1, QUP), send(line1, QDOWN)
    left = halve(left, send(left[1:], XIN), line1)[0]
    left = left + send(left, PIN)
    left = left + send(left, POUT)
    left = send(left, CORE)
    top0 = tie(top0, left, bottom0)
    opposite0 = send(top0, QUP)
    left = left + send(left, PIN)
    left = left + send(left, POUT)
    left = left[None]
    left = cat(left, send(left, XIN))
    left = cat(left, send(left, XOUT))
    left = cat(send(left, CORE), left)

    basis, six, inverse = make_basis(by_rep, left)
    part = errors_right(by_rep, left, errors)
    kept = arrange(by_ring, output_grads)
    w = project(by_rep, left, activations, top0, bottom0)[None]
    w = send(w, CORE)
    w = cat(w, send(w, PIN))
    w = pair(w, send(w, POUT), inverse)
    w = send(w, CORE)
    sum0 = add_rows(errors, 0, ((line0, 0), (top0, 1), (bottom0, 2)), kept, 0, PART)
    bottom1 = tie(bottom1, w, sum0)
    opposite1 = send(bottom1, QDOWN)
    sum1 = add_rows(errors, PART // STRIP, ((line1, 0), (bottom1, 2)), kept, 0, PART)
    w = pair(w, send(w, PIN), part, sum0, opposite0)
    w = cat(w, send(w, POUT))
    right = right_terms(in_kept, w, part, inverse, kept)
    for perm in (CORE, XIN, XOUT):
        right = right + send(right, perm)
    update = (six, right)
    out = add_rows(sum0, 0, ((opposite0, 3),), kept, 0, 2 * PART, update)
    out = add_rows(sum1, 0, ((top1, 1), (opposite1, 3)), kept, PART, 2 * PART, update, out)
    return (out[None], basis.T, right.T)


def solution(mesh):
    placed = (
        P(("replica", "shard"), None),
        P("replica", "shard"),
        P("replica", None, "shard"),
        P("shard", None),
    )
    return jax.shard_map(
        local,
        mesh=mesh,
        in_specs=placed,
        out_specs=(P("replica", None, "shard"), P(), P("shard", None)),
        check_vma=False,
    )
```
